128 devices in a mesh: pair: 16 (over z, y), virt: 8 (over x, core).
Axes of the slice: x: 4, y: 4, z: 4, core: 2. Of those that a mesh axis runs over, the one named last changes fastest.
Arguments:
- amplitudes: bfloat16 [1024, 32768], P('pair', 'virt'), may hold values from -6 to 6
- ladder_ints: bfloat16 [32768, 8, 4096], P('virt', None, 'pair'), may hold values from -0.09375 to 0.09375
- hole_ints: bfloat16 [1024, 1024], P('pair'), may hold values from -0.1875 to 0.1875
- tile_irrep: int32 [256], replicated, may hold values from 0 to 7, as said below
- pair_orbitals: int32 [1024, 2], P('pair'), may hold values from 0 to 199
- occ_energy: float32 [200], replicated, may hold values from -3 to -0.3
- pair_energy: float32 [32768], P('virt'), may hold values from 0.5 to 4
Outputs:
- residual: float32 [1024, 32768], P('pair', 'virt')
- update: bfloat16 [1024, 32768], P('pair', 'virt')
The draws below stay inside these ranges and needn't reach their ends.
Inputs may be any that keep to these rules, and one draw needn't show every extreme that they name: `tile_irrep`: each aligned block of 8 consecutive tiles holds every label exactly once.
All inputs are finite; a program needn't handle non-finite values.
Results may differ from the reference program's by a relative error of at most 0.001.
Values may be sent and summed in bfloat16 or wider, within the bound.
No kernel may reach another device: no remote copies, remote signals or barrier semaphores. Data moves between devices by JAX's collectives and lax.ppermute only.
A program may use at most 192 MiB of HBM per device.

```python
import jax
import jax.numpy as jnp
from jax import lax

TW = 128
IRREPS = 8
NOCC = 200
PAIRS = 1024
NTILES = 256
COLS = 32768
N_VIRT = 8


def draw_tile_irrep(key, part):
    key = jax.random.fold_in(key, 11)
    blocks = NTILES // IRREPS
    keys = jax.random.split(key, blocks)
    perms = jax.vmap(lambda k: jax.random.permutation(k, IRREPS))(keys)
    return perms.reshape(NTILES).astype(jnp.int32)


def with_ends(result, own_key, low, top_value):
    spot = [jax.random.randint(jax.random.fold_in(own_key, axis), (), 0, length) for axis, length in enumerate(result.shape)]
    longest = result.shape.index(max(result.shape))
    next_to = spot[:longest] + [(spot[longest] + 1) % result.shape[longest]] + spot[longest + 1:]
    return result.at[tuple(spot)].set(low).at[tuple(next_to)].set(top_value)


def level_of(own_key, shape, cuts, least, largest):
    def one(position, blocks):
        steps = jax.random.uniform(jax.random.fold_in(jax.random.fold_in(own_key, 6), position), (blocks,), jnp.float32, least / len(cuts), largest / len(cuts))
        return jnp.repeat(jnp.exp(steps), shape[position] // blocks).reshape((-1,) + (1,) * (len(shape) - position - 1))

    level = one(*cuts[0])
    for cut in cuts[1:]:
        level = level * one(*cut)
    return level


def centred(rng, dims, deviation, most, shards=(), held_as=jnp.bfloat16):
    drawn = jax.random.normal(rng, dims, jnp.float32) * deviation
    if len(shards) > 0:
        drawn = level_of(rng, dims, shards, -0.22, 0.18) * drawn
    return jnp.clip(drawn, min=-most, max=most).astype(held_as)


def setup_inputs(seed: int = 0) -> dict:
    arg_keys = jax.random.split(jax.random.key(seed), 8)
    return {
        "amplitudes": centred(arg_keys[0], (PAIRS, COLS), 1.0, 6.0, ((0, 16), (1, 8))),
        "ladder_ints": centred(arg_keys[1], (COLS, N_VIRT, COLS // N_VIRT), (COLS // IRREPS) ** -0.5, 0.09375, ((0, 8), (2, 16))),
        "hole_ints": centred(arg_keys[2], (PAIRS, PAIRS), PAIRS ** -0.5, 0.1875, ((0, 16),)),
        "tile_irrep": draw_tile_irrep(jax.random.fold_in(arg_keys[7], 71), 0),
        "pair_orbitals": with_ends(jax.random.randint(arg_keys[4], (PAIRS, 2), 0, NOCC), jax.random.fold_in(arg_keys[4], 1), 0, NOCC - 1).astype(jnp.int32),
        "occ_energy": jnp.clip(jax.random.uniform(arg_keys[5], (NOCC,), jnp.float32, -3.0, -0.3), -3.0, -0.3),
        "pair_energy": jnp.clip(0.5 + 3.5 * jax.random.uniform(arg_keys[6], (COLS,), jnp.float32) ** level_of(arg_keys[6], (COLS,), ((0, 8),), -0.2, 0.2), 0.5, 4.0),
    }


def reference(amplitudes, ladder_ints, hole_ints, tile_irrep, pair_orbitals, occ_energy, pair_energy):
    cols = amplitudes.shape[1]
    pairs = amplitudes.shape[0]
    blk = cols // N_VIRT
    ints = ladder_ints.reshape(cols, cols)
    col_irrep = jnp.repeat(tile_irrep, TW)

    def step(total, index):
        start = (index * blk).astype(jnp.int32)
        rows = lax.dynamic_slice_in_dim(ints, start, blk, 0)
        labels = lax.dynamic_slice_in_dim(col_irrep, start, blk, 0)
        keep = (labels[:, None] == col_irrep[None, :]).astype(ints.dtype)
        piece = lax.dynamic_slice_in_dim(amplitudes, start, blk, 1)
        return total + jnp.dot(piece, rows * keep, preferred_element_type=jnp.float32), None

    particle, _ = lax.scan(step, jnp.zeros((pairs, cols), jnp.float32), jnp.arange(N_VIRT, dtype=jnp.int32))
    hole = jnp.dot(hole_ints, amplitudes, preferred_element_type=jnp.float32)
    residual = particle + hole
    occupied = occ_energy[pair_orbitals[:, 0]] + occ_energy[pair_orbitals[:, 1]]
    denom = pair_energy[None, :] - occupied[:, None]
    update = (residual / denom).astype(jnp.bfloat16)
    return residual, update
```

```python
import functools

import jax
import jax.numpy as jnp
from jax import lax
from jax.experimental import pallas as pl
from jax.experimental.pallas import tpu as pltpu
from jax.sharding import Mesh
from jax.sharding import PartitionSpec as P

TW = 128
RING = 4
AXES = ("z", "y", "x", "core")
BF = jnp.bfloat16
F32 = jnp.float32
VMEM_LIMIT = 48 * 1024 * 1024
RELS = (0, -1, 1, 2)


def flat(z, y, x, c):
    return (((z % RING) * RING + y % RING) * RING + x % RING) * 2 + c


def perm_of(first, step):
    pairs = []
    for z in range(RING):
        for y in range(RING):
            for x in range(RING):
                for c in range(2):
                    if (c == 0) == first:
                        to = flat(z, y + step, x, c)
                    else:
                        to = flat(z + step, y, x, c)
                    pairs.append((flat(z, y, x, c), to))
    return pairs


def along(value, first, step):
    return lax.ppermute(value, AXES, perm_of(first, step))


def along_x(value, step):
    return lax.ppermute(value, "x", [(i, (i + step) % RING) for i in range(RING)])


def other_core(value):
    return lax.ppermute(value, "core", [(0, 1), (1, 0)])


def select_kernel(tab, *refs):
    blocks, out = refs[:4], refs[4]
    o = tab[pl.program_id(0) * 16 + 8]
    row = lax.broadcasted_iota(jnp.int32, (TW, 8 * TW), 0)
    col = lax.broadcasted_iota(jnp.int32, (TW, 8 * TW), 1)
    pick = jnp.where(col == row * 8 + o, 1.0, 0.0).astype(BF)
    for k in range(4):
        got = jnp.dot(pick, blocks[k][...], preferred_element_type=F32)
        out[0, k * TW:(k + 1) * TW, :] = got.astype(BF)


def select(tab, ints2d):
    specs = [
        pl.BlockSpec((8 * TW, TW), functools.partial(lambda i, t, k: (t[i * 16 + k], i % 2), k=k))
        for k in range(4)
    ]
    return pl.pallas_call(
        select_kernel,
        grid_spec=pltpu.PrefetchScalarGridSpec(
            num_scalar_prefetch=1,
            grid=(16,),
            in_specs=specs,
            out_specs=pl.BlockSpec((1, 4 * TW, TW), lambda i, t: (i, 0, 0)),
        ),
        out_shape=jax.ShapeDtypeStruct((16, 4 * TW, TW), BF),
        compiler_params=pltpu.CompilerParams(vmem_limit_bytes=VMEM_LIMIT),
        cost_estimate=pl.CostEstimate(
            flops=64 * 2 * TW * TW * 8 * TW, bytes_accessed=18 * 2**20, transcendentals=0
        ),
        name="select",
    )(tab, *([ints2d] * 4))


def ladder_kernel(tab, *refs, pieces):
    n = len(pieces)
    a_refs, w_refs, outs = refs[:n], refs[n:n + 2], refs[n + 2:n + 6]
    a_v, w_v, a_sem, w_sem = refs[n + 6:]
    copies = []
    at = 0
    for i in range(n):
        copies.append(
            pltpu.make_async_copy(a_refs[i], a_v.at[pl.ds(at, pieces[i])], a_sem.at[i])
        )
        at += pieces[i]
    w_copies = [
        [
            pltpu.make_async_copy(
                w_refs[s].at[pl.ds(4 * d, 4)], w_v.at[s, pl.ds(4 * d, 4)], w_sem.at[s, d]
            )
            for s in range(2)
        ]
        for d in range(RING)
    ]
    for cp in copies:
        cp.start()
    for pair in w_copies:
        for cp in pair:
            cp.start()
    for cp in copies:
        cp.wait()
    for d in range(RING):
        for cp in w_copies[d]:
            cp.wait()
        for q in range(4):
            ct = d * 4 + q
            cols = [
                a_v[:, pl.ds(pl.multiple_of(tab[ct * 16 + m] * TW, TW), TW)] for m in range(8)
            ]
            a = jnp.concatenate(cols, axis=1)
            w = jnp.concatenate([w_v[0, ct], w_v[1, ct ^ 2]], axis=0)
            outs[d][:, q * TW:(q + 1) * TW] = jnp.dot(a, w, preferred_element_type=F32)


def ladder(tab, a_list, w_own, w_other):
    pieces = tuple(a.shape[0] for a in a_list)
    rows, cols = sum(pieces), a_list[0].shape[1]
    n = len(pieces)
    return pl.pallas_call(
        functools.partial(ladder_kernel, pieces=pieces),
        in_specs=[pl.BlockSpec(memory_space=pltpu.SMEM)] + [pl.BlockSpec(memory_space=pl.ANY)] * (n + 2),
        out_specs=[pl.BlockSpec(memory_space=pltpu.VMEM)] * RING,
        out_shape=[jax.ShapeDtypeStruct((rows, 4 * TW), F32)] * RING,
        scratch_shapes=[
            pltpu.VMEM((rows, cols), BF),
            pltpu.VMEM((2, 16, 4 * TW, TW), BF),
            pltpu.SemaphoreType.DMA((n,)),
            pltpu.SemaphoreType.DMA((2, RING)),
        ],
        compiler_params=pltpu.CompilerParams(vmem_limit_bytes=VMEM_LIMIT),
        cost_estimate=pl.CostEstimate(
            flops=16 * 2 * rows * 8 * TW * TW, bytes_accessed=rows * cols * 2 + rows * 8192 + 4 * 2**20, transcendentals=0
        ),
        name="ladder",
    )(tab, *a_list, w_own, w_other)


def hole_kernel(h_ref, *refs):
    n = (len(refs) - 2) // 2
    for out, parts in ((refs[-2], refs[:n]), (refs[-1], refs[n:2 * n])):
        a = jnp.concatenate([r[...] for r in parts], axis=0)
        out[...] = jnp.dot(h_ref[...], a, preferred_element_type=F32)


def hole_part(h_rel, a_list, width):
    step = 1024
    steps = width // step
    rows = h_rel.shape[0]
    specs = [pl.BlockSpec((a.shape[0], step), lambda i: (0, i)) for a in a_list]
    specs2 = [pl.BlockSpec((a.shape[0], step), lambda i: (0, i + steps)) for a in a_list]
    return pl.pallas_call(
        hole_kernel,
        grid=(steps,),
        in_specs=[pl.BlockSpec(h_rel.shape, lambda i: (0, 0))] + specs + specs2,
        out_specs=[pl.BlockSpec((rows, step), lambda i: (0, i))] * 2,
        out_shape=[jax.ShapeDtypeStruct((rows, width), F32)] * 2,
        compiler_params=pltpu.CompilerParams(vmem_limit_bytes=VMEM_LIMIT),
        cost_estimate=pl.CostEstimate(
            flops=2 * rows * h_rel.shape[1] * 2 * width, bytes_accessed=10 * 2**20, transcendentals=0
        ),
        name="hole",
    )(h_rel, *a_list, *a_list)


def finish_kernel(where, keep0, keep1, keep2, keep3, got, hole_a, hole_b, occ, energy, res, upd):
    core = where[32]
    mine = pl.multiple_of(core * 32, 32)
    his = pl.multiple_of((1 - core) * 32, 32)
    keeps = (keep0, keep1, keep2, keep3)
    for i in range(16):
        for first, part, at in ((mine, keeps[i // 4][i % 4, :, :256], i), (his, got[i], 16 + i)):
            rows = pl.ds(first, 32)
            cols = pl.ds(pl.multiple_of(where[at] * 256, 256), 256)
            total = part + (hole_a[rows, cols] + hole_b[rows, cols])
            res[rows, cols] = total
            upd[rows, cols] = (total / (energy[:, cols] - occ[rows, :])).astype(BF)


def finish(where, keeps, got, hole_a, hole_b, occ, energy):
    shape = hole_a.shape
    vm = pl.BlockSpec(memory_space=pltpu.VMEM)
    return pl.pallas_call(
        finish_kernel,
        in_specs=[pl.BlockSpec(memory_space=pltpu.SMEM)] + [vm] * 9,
        out_specs=[vm, vm],
        out_shape=[jax.ShapeDtypeStruct(shape, F32), jax.ShapeDtypeStruct(shape, BF)],
        compiler_params=pltpu.CompilerParams(vmem_limit_bytes=VMEM_LIMIT),
        cost_estimate=pl.CostEstimate(flops=2**20, bytes_accessed=6 * 2**20, transcendentals=0),
        name="finish",
    )(where, *keeps, got, hole_a, hole_b, occ, energy)


def local(amplitudes, ladder_ints, hole_ints, tile_irrep, pair_orbitals, occ_energy, pair_energy):
    z, y, x, c = (lax.axis_index(name) for name in AXES)
    rows, width = amplitudes.shape
    half = rows // 2
    p = z * RING + y

    mine = lax.dynamic_slice_in_dim(amplitudes, c * half, half, 0)
    theirs = other_core(lax.dynamic_slice_in_dim(amplitudes, (1 - c) * half, half, 0))
    own = jnp.concatenate([mine, theirs], axis=1)

    i = jnp.arange(16, dtype=jnp.int32)
    rel = sum(jnp.where(i // 4 == k, jnp.int32(RELS[k] % RING), 0) for k in range(RING))
    o = 2 * ((x + rel) % RING) + (c + i // 2 % 2) % 2
    tile = o * 32 + 2 * p + i % 2
    t = jnp.arange(tile_irrep.shape[0], dtype=jnp.int32)
    label = jnp.sum(jnp.where(tile[:, None] == t[None, :], tile_irrep[None, :], 0), axis=1)
    m = jnp.arange(16, dtype=jnp.int32)
    v_of = 2 * x + (c + m // 4) % 2
    block = v_of * 4 + m % 4
    hit = (t[None, None, :] // 8 == block[None, :, None]) & (tile_irrep[None, None, :] == label[:, None, None])
    inside = jnp.sum(jnp.where(hit, t[None, None, :] % 8, 0), axis=2)
    offs = (m // 4 * 32 + m % 4 * 8)[None, :] + inside
    tab = jnp.where(m[None, :] < 8, offs, o[:, None]).reshape(256)

    w_own = select(tab, ladder_ints.reshape(-1, ladder_ints.shape[2]))
    w_other = other_core(w_own)

    r_m = along(own, True, 1)
    r_p = along(own, True, -1)
    s_a = jnp.concatenate([own, r_m], axis=0)
    r_2a = along(r_m[:half // 2], True, 1)
    r_2b = along(r_p[half // 2:], True, -1)
    s_b = jnp.concatenate([r_p, r_2a, r_2b], axis=0)
    q_ma = along(s_a, False, 1)
    q_pa = along(s_a, False, -1)
    q_mb = along(s_b, False, 1)
    q_pb = along(s_b, False, -1)
    q_2a = along(q_ma, False, 1)
    q_2b = along(q_pb, False, -1)
    a_list = [s_a, s_b, q_ma, q_mb, q_pa, q_pb, q_2a, q_2b]

    def summed(parts):
        out = ladder(tab, parts, w_own, w_other)
        return [out[0]] + [along_x(out[k], RELS[k]) for k in range(1, RING)]

    c1 = summed([s_a, s_b])
    c2 = summed([q_ma, q_mb, q_pa, q_pb])
    c3 = summed([q_2a, q_2b])
    block_rows = RING * half
    t_0 = sum(c1[1:], c1[0])
    t_m = sum((part[:block_rows] for part in c2[1:]), c2[0][:block_rows])
    t_p = sum((part[block_rows:] for part in c2[1:]), c2[0][block_rows:])
    t_2 = sum(c3[1:], c3[0])

    from_p = along(t_m, False, -1)
    from_m = along(t_p, False, 1)
    from_2 = along(t_2, False, 2)
    back = [t_0, from_m, from_p, from_2]
    keeps = []
    for k in range(RING):
        u = jnp.stack([b[k * half:(k + 1) * half] for b in back])
        keeps.append(u if k == 0 else along(u, True, RELS[k]))
    got = other_core(jnp.concatenate([u[:, :, 256:] for u in keeps], axis=0))

    j = jnp.arange(16 * half, dtype=jnp.int32)
    ds = sum(jnp.where(j // (4 * half) == k, jnp.int32(RELS[k] % RING), 0) for k in range(RING))
    df = sum(jnp.where(j // half % 4 == k, jnp.int32(RELS[k] % RING), 0) for k in range(RING))
    dz, dy = jnp.where(c == 0, ds, df), jnp.where(c == 0, df, ds)
    source = ((z + dz) % RING * RING + (y + dy) % RING) * rows + c * half + j % half
    onehot = (jnp.arange(hole_ints.shape[1], dtype=jnp.int32)[:, None] == source[None, :]).astype(BF)
    h_rel = jnp.dot(hole_ints, onehot, preferred_element_type=F32).astype(BF)
    hole_own, hole_send = hole_part(h_rel, a_list, width)
    hole_got = other_core(hole_send)

    i = jnp.arange(33, dtype=jnp.int32)
    kf = sum(jnp.where(i // 4 % 4 == k, jnp.int32(-RELS[k] % RING), 0) for k in range(RING))
    ks = sum(jnp.where(i % 4 == k, jnp.int32(RELS[k] % RING), 0) for k in range(RING))
    flip = (c + i // 16) % 2 == 0
    kz, ky = jnp.where(flip, ks, kf), jnp.where(flip, kf, ks)
    where = jnp.where(i == 32, c, (z + kz) % RING * RING + (y + ky) % RING)

    orbital = jnp.arange(occ_energy.shape[0], dtype=jnp.int32)
    picked = (pair_orbitals[:, :, None] == orbital[None, None, :]).astype(F32)
    occ = jnp.sum(picked * occ_energy[None, None, :], axis=(1, 2))[:, None]
    return finish(where, keeps, got, hole_own, hole_got, occ, pair_energy[None, :])


def solution(mesh):
    grid = Mesh(mesh.devices.reshape(RING, RING, RING, 2), AXES)
    pair, virt = ("z", "y"), ("x", "core")
    placed = (
        P(pair, virt),
        P(virt, None, pair),
        P(pair, None),
        P(),
        P(pair, None),
        P(),
        P(virt),
    )
    return jax.shard_map(
        local,
        mesh=grid,
        in_specs=placed,
        out_specs=(P(pair, virt), P(pair, virt)),
        check_vma=False,
    )
```

```python
import functools

import jax
import jax.numpy as jnp
from jax import lax
from jax.experimental import pallas as pl
from jax.experimental.pallas import tpu as pltpu
from jax.sharding import Mesh
from jax.sharding import PartitionSpec as P

TW = 128
RING = 4
AXES = ("z", "y", "x", "core")
BF = jnp.bfloat16
F32 = jnp.float32
VMEM_LIMIT = 24 * 1024 * 1024
SCALE = 64.0
F16 = jnp.float16
LIGHT = pl.CostEstimate(flops=1024, bytes_accessed=1024, transcendentals=0)
RELS = (0, -1, 1, 2)


def flat(z, y, x, c):
    return (((z % RING) * RING + y % RING) * RING + x % RING) * 2 + c


def perm_of(first, step):
    pairs = []
    for z in range(RING):
        for y in range(RING):
            for x in range(RING):
                for c in range(2):
                    if (c == 0) == first:
                        to = flat(z, y + step, x, c)
                    else:
                        to = flat(z + step, y, x, c)
                    pairs.append((flat(z, y, x, c), to))
    return pairs


def along(value, first, step):
    return lax.ppermute(value, AXES, perm_of(first, step))


def partner(x, c, first):
    return x ^ 1 if (c == 0) == first else RING - 1 - x


def across_x(value, first):
    pairs = []
    for z in range(RING):
        for y in range(RING):
            for x in range(RING):
                for c in range(2):
                    pairs.append((flat(z, y, x, c), flat(z, y, partner(x, c, first), c)))
    return lax.ppermute(value, AXES, pairs)


def other_core(value):
    return lax.ppermute(value, "core", [(0, 1), (1, 0)])


def select_kernel(tab, ints, out, held, sem, *, first_block):
    rows = 8 * 8 * TW
    copies = [
        pltpu.make_async_copy(ints.at[pl.ds((first_block + b) * rows, rows)], held.at[b], sem.at[b])
        for b in range(2)
    ]
    for cp in copies:
        cp.start()
    row = lax.broadcasted_iota(jnp.int32, (32, 256), 0)
    col = lax.broadcasted_iota(jnp.int32, (32, 256), 1)
    for b in range(2):
        copies[b].wait()
        for ct in range(16):
            pick = jnp.where(col == row * 8 + tab[ct * 16 + 8], 1.0, 0.0).astype(BF)
            tile = tab[ct * 16 + first_block + b] - (first_block + b) * 8
            for g in range(4):
                at = pl.multiple_of(tile * 8 * TW + g * 256, 256)
                got = jnp.dot(
                    pick, held[b, pl.ds(at, 256), ct % 2 * TW:(ct % 2 + 1) * TW], preferred_element_type=F32
                )
                out[ct, b * TW + g * 32:b * TW + (g + 1) * 32, :] = got.astype(BF)


def select(tab, ints2d, first_block):
    return pl.pallas_call(
        functools.partial(select_kernel, first_block=first_block),
        in_specs=[pl.BlockSpec(memory_space=pltpu.SMEM), pl.BlockSpec(memory_space=pltpu.HBM)],
        out_specs=pl.BlockSpec(memory_space=pltpu.VMEM),
        out_shape=jax.ShapeDtypeStruct((16, 2 * TW, TW), BF),
        scratch_shapes=[pltpu.VMEM((2, 8 * 8 * TW, 2 * TW), BF), pltpu.SemaphoreType.DMA((2,))],
        compiler_params=pltpu.CompilerParams(vmem_limit_bytes=50 * 1024 * 1024),
        cost_estimate=LIGHT,
        name="select",
    )(tab, ints2d)


def ladder_kernel(tab, *refs, n):
    a_refs, w_own, w_other, outs = refs[:n], refs[n:n + 2], refs[n + 2:n + 4], refs[n + 4:]
    for ct in range(16):
        d, q = ct // 4, ct % 4
        cols = [
            jnp.concatenate(
                [a[:, pl.ds(pl.multiple_of(tab[ct * 16 + m] * TW, TW), TW)] for a in a_refs], axis=0
            )
            for m in range(8)
        ]
        there = (0, 2, 1, 3)[d] * 4 + (q ^ 2)
        w = jnp.concatenate([w[ct] for w in w_own] + [w[there] for w in w_other], axis=0)
        got = jnp.dot(jnp.concatenate(cols, axis=1), w, preferred_element_type=F32)
        at = d % 2 * 4 + q
        outs[d // 2][:, at * TW:(at + 1) * TW] = got


def ladder(tab, a_list, w_own, w_other):
    rows, n = sum(a.shape[0] for a in a_list), len(a_list)
    vm = pl.BlockSpec(memory_space=pltpu.VMEM)
    return pl.pallas_call(
        functools.partial(ladder_kernel, n=n),
        in_specs=[pl.BlockSpec(memory_space=pltpu.SMEM)] + [vm] * (n + 4),
        out_specs=[vm] * 2,
        out_shape=[jax.ShapeDtypeStruct((rows, 8 * TW), F32)] * 2,
        compiler_params=pltpu.CompilerParams(vmem_limit_bytes=VMEM_LIMIT),
        cost_estimate=LIGHT,
        name="ladder",
    )(tab, *a_list, *w_own, *w_other)


def hole_kernel(h_ref, *refs):
    n = (len(refs) - 2) // 2
    for out, parts in ((refs[-2], refs[:n]), (refs[-1], refs[n:2 * n])):
        a = jnp.concatenate([r[...] for r in parts], axis=0)
        out[...] = jnp.dot(h_ref[...], a, preferred_element_type=F32)


def hole_part(h_rel, a_list, width):
    step = 1024
    steps = width // step
    rows = h_rel.shape[0]
    specs = [pl.BlockSpec((a.shape[0], step), lambda i: (0, i)) for a in a_list]
    specs2 = [pl.BlockSpec((a.shape[0], step), lambda i: (0, i + steps)) for a in a_list]
    return pl.pallas_call(
        hole_kernel,
        grid=(steps,),
        in_specs=[pl.BlockSpec(h_rel.shape, lambda i: (0, 0))] + specs + specs2,
        out_specs=[pl.BlockSpec((rows, step), lambda i: (0, i))] * 2,
        out_shape=[jax.ShapeDtypeStruct((rows, width), F32)] * 2,
        compiler_params=pltpu.CompilerParams(vmem_limit_bytes=VMEM_LIMIT),
        cost_estimate=LIGHT,
        name="hole",
    )(h_rel, *a_list, *a_list)


def finish_kernel(where, *refs):
    keeps, (got, hole_a, hole_b, occ, energy, res, upd) = refs[:RING], refs[RING:]
    core = where[32]
    mine = pl.multiple_of(core * 32, 32)
    his = pl.multiple_of((1 - core) * 32, 32)
    for i in range(16):
        own = keeps[i // 4][i % 4 * 32:(i % 4 + 1) * 32, :256]
        for first, part, at in ((mine, own, i), (his, got[i * 32:(i + 1) * 32], 16 + i)):
            rows = pl.ds(first, 32)
            cols = pl.ds(pl.multiple_of(where[at] * 256, 256), 256)
            total = part + (hole_a[rows, cols] + hole_b[rows, cols])
            res[rows, cols] = total
            upd[rows, cols] = (total / (energy[:, cols] - occ[rows, :])).astype(BF)


def finish(where, keeps, got, hole_a, hole_b, occ, energy):
    shape = hole_a.shape
    vm = pl.BlockSpec(memory_space=pltpu.VMEM)
    return pl.pallas_call(
        finish_kernel,
        in_specs=[pl.BlockSpec(memory_space=pltpu.SMEM)] + [vm] * 9,
        out_specs=[vm, vm],
        out_shape=[jax.ShapeDtypeStruct(shape, F32), jax.ShapeDtypeStruct(shape, BF)],
        compiler_params=pltpu.CompilerParams(vmem_limit_bytes=VMEM_LIMIT),
        cost_estimate=LIGHT,
        name="finish",
    )(where, *keeps, got, hole_a, hole_b, occ, energy)


def local(amplitudes, ladder_ints, hole_ints, tile_irrep, pair_orbitals, occ_energy, pair_energy):
    z, y, x, c = (lax.axis_index(name) for name in AXES)
    rows, width = amplitudes.shape
    half = rows // 2
    p = z * RING + y

    mine = lax.dynamic_slice_in_dim(amplitudes, c * half, half, 0)
    theirs = other_core(lax.dynamic_slice_in_dim(amplitudes, (1 - c) * half, half, 0))
    own = jnp.concatenate([mine, theirs], axis=1)

    i = jnp.arange(16, dtype=jnp.int32)
    low, high = x ^ 1, RING - 1 - x
    first, second = jnp.where(c == 0, low, high), jnp.where(c == 0, high, low)
    goes = jnp.where(i < 4, x, jnp.where(i < 8, second, jnp.where(i < 12, first, (x + 2) % RING)))
    o = 2 * goes + (c + i // 2 % 2) % 2
    tile = o * 32 + 2 * p + i % 2
    t = jnp.arange(tile_irrep.shape[0], dtype=jnp.int32)
    label = jnp.sum(jnp.where(tile[:, None] == t[None, :], tile_irrep[None, :], 0), axis=1)
    m = jnp.arange(16, dtype=jnp.int32)
    v_of = 2 * x + (c + m // 4) % 2
    block = v_of * 4 + m % 4
    hit = (t[None, None, :] // 8 == block[None, :, None]) & (tile_irrep[None, None, :] == label[:, None, None])
    inside = jnp.sum(jnp.where(hit, t[None, None, :] % 8, 0), axis=2)
    offs = (m // 4 * 32 + m % 4 * 8)[None, :] + inside
    tab = jnp.where(m[None, :] < 8, offs, o[:, None]).reshape(256)

    hold = lax.optimization_barrier
    ints2d = ladder_ints.reshape(-1, ladder_ints.shape[2])

    quarter = half // 2
    r_m = along(own, True, 1)
    r_p = along(own, True, -1)
    w_a = select(hold((tab, own))[0], ints2d, 0)
    r_m, r_p, w_a, tab = hold((r_m, r_p, w_a, tab))
    s_a = jnp.concatenate([own, r_m, r_p[:quarter]], axis=0)
    q_ma = along(s_a, False, 1)
    q_pa = along(s_a, False, -1)
    r_2a = along(r_m[:quarter], True, 1)
    r_2b = along(r_p[quarter:], True, -1)
    w_b = select(tab, ints2d, 2)
    r_2a, r_2b, w_b = hold((r_2a, r_2b, w_b))
    s_b = jnp.concatenate([r_p[quarter:], r_2a, r_2b], axis=0)
    q_mb = along(s_b, False, 1)
    q_pb = along(s_b, False, -1)
    w_own = [w_a, w_b]
    w_other = [other_core(w) for w in w_own]

    i = jnp.arange(33, dtype=jnp.int32)
    kf = sum(jnp.where(i // 4 % 4 == k, jnp.int32(-RELS[k] % RING), 0) for k in range(RING))
    ks = sum(jnp.where(i % 4 == k, jnp.int32(RELS[k] % RING), 0) for k in range(RING))
    flip = (c + i // 16) % 2 == 0
    kz, ky = jnp.where(flip, ks, kf), jnp.where(flip, kf, ks)
    where = jnp.where(i == 32, c, (z + kz) % RING * RING + (y + ky) % RING)
    orbital = jnp.arange(occ_energy.shape[0], dtype=jnp.int32)
    picked = (pair_orbitals[:, :, None] == orbital[None, None, :]).astype(F32)
    occ = jnp.sum(picked * occ_energy[None, None, :], axis=(1, 2))[:, None]

    j = jnp.arange(16 * half, dtype=jnp.int32)
    ds = sum(jnp.where(j // (4 * half) == k, jnp.int32(RELS[k] % RING), 0) for k in range(RING))
    df = sum(jnp.where(j // half % 4 == k, jnp.int32(RELS[k] % RING), 0) for k in range(RING))
    dz, dy = jnp.where(c == 0, ds, df), jnp.where(c == 0, df, ds)
    source = ((z + dz) % RING * RING + (y + dy) % RING) * rows + c * half + j % half
    onehot = (jnp.arange(hole_ints.shape[1], dtype=jnp.int32)[:, None] == source[None, :]).astype(BF)
    h_rel = jnp.dot(hole_ints, onehot, preferred_element_type=F32).astype(BF)

    q_ma, q_pa, w_other, where, occ, h_rel = hold((q_ma, q_pa, w_other, where, occ, h_rel))
    q_2a = along(q_ma, False, 1)
    q_2b = along(q_pb, False, -1)
    a_list = [s_a, s_b, q_ma, q_mb, q_pa, q_pb, q_2a, q_2b]

    mid = 4 * TW
    block = RING * half

    def coded(value):
        return (value * SCALE).astype(F16)

    def decoded(value):
        return value.astype(F32) * (1.0 / SCALE)

    keep_0, send_0 = ladder(tab, a_list[:2], w_own, w_other)
    q_mb, q_pb, keep_0, send_0 = hold((q_mb, q_pb, keep_0, send_0))
    keep_1, send_1 = ladder(tab, [q_ma, q_mb, q_pa, q_pb], w_own, w_other)
    near_got = across_x(jnp.concatenate([coded(send_0), coded(send_1)], axis=0), True)
    keep_2, send_2 = ladder(tab, a_list[6:], w_own, w_other)
    far_send = coded(send_2)
    far_got = across_x(far_send, True)
    near_got, _ = hold((near_got, far_send))
    sum_0 = keep_0 + decoded(near_got[:block])
    sum_1 = keep_1 + decoded(near_got[block:])
    near_end = across_x(jnp.concatenate([coded(sum_0[:, mid:]), coded(sum_1[:, mid:])], axis=0), False)
    sum_2 = keep_2 + decoded(far_got)
    far_end = across_x(coded(sum_2[:, mid:]), False)
    near_end, h_rel = hold((near_end, h_rel))
    t_0 = sum_0[:, :mid] + decoded(near_end[:block])
    t_m = sum_1[:block, :mid] + decoded(near_end[block:2 * block])
    t_p = sum_1[block:, :mid] + decoded(near_end[2 * block:])
    t_2 = sum_2[:, :mid] + decoded(far_end)

    from_p = along(t_m, False, -1)
    from_m = along(t_p, False, 1)
    from_2 = along(t_2, False, 2)
    hole_own, hole_send = hole_part(h_rel, a_list, width)
    from_p, from_m, from_2, hole_send = hold((from_p, from_m, from_2, hole_send))
    hole_got = other_core(hole_send)
    back = [t_0, from_m, from_p, from_2]
    keeps = []
    for k in range(RING):
        u = jnp.concatenate([part[k * half:(k + 1) * half] for part in back], axis=0)
        keeps.append(u if k == 0 else along(u, True, RELS[k]))
    got = other_core(jnp.concatenate([u[:, mid // 2:] for u in keeps], axis=0))
    return finish(where, keeps, got, hole_own, hole_got, occ, pair_energy[None, :])


def solution(mesh):
    grid = Mesh(mesh.devices.reshape(RING, RING, RING, 2), AXES)
    pair, virt = ("z", "y"), ("x", "core")
    placed = (
        P(pair, virt),
        P(virt, None, pair),
        P(pair, None),
        P(),
        P(pair, None),
        P(),
        P(virt),
    )
    return jax.shard_map(
        local,
        mesh=grid,
        in_specs=placed,
        out_specs=(P(pair, virt), P(pair, virt)),
        check_vma=False,
    )
```

```python
import functools

import jax
import jax.numpy as jnp
from jax import lax
from jax.experimental import pallas as pl
from jax.experimental.pallas import tpu as pltpu
from jax.sharding import Mesh
from jax.sharding import PartitionSpec as P

TW = 128
RING = 4
AXES = ("z", "y", "x", "core")
BF = jnp.bfloat16
F32 = jnp.float32
VMEM_LIMIT = 24 * 1024 * 1024
SCALE = 64.0
F16 = jnp.float16
HEAVY = pl.CostEstimate(flops=2**36, bytes_accessed=2**26, transcendentals=0)
LIGHT = pl.CostEstimate(flops=1024, bytes_accessed=1024, transcendentals=0)
RELS = (0, -1, 1, 2)


def flat(z, y, x, c):
    return (((z % RING) * RING + y % RING) * RING + x % RING) * 2 + c


def perm_of(first, step):
    pairs = []
    for z in range(RING):
        for y in range(RING):
            for x in range(RING):
                for c in range(2):
                    if (c == 0) == first:
                        to = flat(z, y + step, x, c)
                    else:
                        to = flat(z + step, y, x, c)
                    pairs.append((flat(z, y, x, c), to))
    return pairs


def along(value, first, step):
    return lax.ppermute(value, AXES, perm_of(first, step))


def partner(x, c, first):
    return x ^ 1 if (c == 0) == first else RING - 1 - x


def across_x(value, first):
    pairs = []
    for z in range(RING):
        for y in range(RING):
            for x in range(RING):
                for c in range(2):
                    pairs.append((flat(z, y, x, c), flat(z, y, partner(x, c, first), c)))
    return lax.ppermute(value, AXES, pairs)


def other_core(value):
    return lax.ppermute(value, "core", [(0, 1), (1, 0)])


def select_kernel(tab, ints, out, held, sem, *, first_block):
    rows = 8 * 8 * TW
    copies = [
        pltpu.make_async_copy(ints.at[pl.ds((first_block + b) * rows, rows)], held.at[b], sem.at[b])
        for b in range(2)
    ]
    for cp in copies:
        cp.start()
    row = lax.broadcasted_iota(jnp.int32, (32, 256), 0)
    col = lax.broadcasted_iota(jnp.int32, (32, 256), 1)
    for b in range(2):
        copies[b].wait()
        for ct in range(16):
            pick = jnp.where(col == row * 8 + tab[ct * 16 + 8], 1.0, 0.0).astype(BF)
            tile = tab[ct * 16 + first_block + b] - (first_block + b) * 8
            for g in range(4):
                at = pl.multiple_of(tile * 8 * TW + g * 256, 256)
                got = jnp.dot(
                    pick, held[b, pl.ds(at, 256), ct % 2 * TW:(ct % 2 + 1) * TW], preferred_element_type=F32
                )
                out[ct, b * TW + g * 32:b * TW + (g + 1) * 32, :] = got.astype(BF)


def select(tab, ints2d, first_block):
    return pl.pallas_call(
        functools.partial(select_kernel, first_block=first_block),
        in_specs=[pl.BlockSpec(memory_space=pltpu.SMEM), pl.BlockSpec(memory_space=pltpu.HBM)],
        out_specs=pl.BlockSpec(memory_space=pltpu.VMEM),
        out_shape=jax.ShapeDtypeStruct((16, 2 * TW, TW), BF),
        scratch_shapes=[pltpu.VMEM((2, 8 * 8 * TW, 2 * TW), BF), pltpu.SemaphoreType.DMA((2,))],
        compiler_params=pltpu.CompilerParams(vmem_limit_bytes=50 * 1024 * 1024),
        cost_estimate=LIGHT,
        name="select",
    )(tab, ints2d)


def ladder_kernel(tab, *refs, n):
    a_refs, w_own, w_other, outs = refs[:n], refs[n:n + 2], refs[n + 2:n + 4], refs[n + 4:]
    for ct in range(16):
        d, q = ct // 4, ct % 4
        cols = [
            jnp.concatenate(
                [a[:, pl.ds(pl.multiple_of(tab[ct * 16 + m] * TW, TW), TW)] for a in a_refs], axis=0
            )
            for m in range(8)
        ]
        there = (0, 2, 1, 3)[d] * 4 + (q ^ 2)
        w = jnp.concatenate([w[ct] for w in w_own] + [w[there] for w in w_other], axis=0)
        got = jnp.dot(jnp.concatenate(cols, axis=1), w, preferred_element_type=F32)
        at = d % 2 * 4 + q
        outs[d // 2][:, at * TW:(at + 1) * TW] = got


def ladder(tab, a_list, w_own, w_other, cost=LIGHT):
    rows, n = sum(a.shape[0] for a in a_list), len(a_list)
    vm = pl.BlockSpec(memory_space=pltpu.VMEM)
    return pl.pallas_call(
        functools.partial(ladder_kernel, n=n),
        in_specs=[pl.BlockSpec(memory_space=pltpu.SMEM)] + [vm] * (n + 4),
        out_specs=[vm] * 2,
        out_shape=[jax.ShapeDtypeStruct((rows, 8 * TW), F32)] * 2,
        compiler_params=pltpu.CompilerParams(vmem_limit_bytes=VMEM_LIMIT),
        cost_estimate=cost,
        name="ladder",
    )(tab, *a_list, *w_own, *w_other)


def hole_kernel(h_ref, *refs):
    n = (len(refs) - 2) // 2
    for out, parts in ((refs[-2], refs[:n]), (refs[-1], refs[n:2 * n])):
        a = jnp.concatenate([r[...] for r in parts], axis=0)
        out[...] = jnp.dot(h_ref[...], a, preferred_element_type=F32)


def hole_part(h_rel, a_list, width):
    step = 1024
    steps = width // step
    rows = h_rel.shape[0]
    specs = [pl.BlockSpec((a.shape[0], step), lambda i: (0, i)) for a in a_list]
    specs2 = [pl.BlockSpec((a.shape[0], step), lambda i: (0, i + steps)) for a in a_list]
    return pl.pallas_call(
        hole_kernel,
        grid=(steps,),
        in_specs=[pl.BlockSpec(h_rel.shape, lambda i: (0, 0))] + specs + specs2,
        out_specs=[pl.BlockSpec((rows, step), lambda i: (0, i))] * 2,
        out_shape=[jax.ShapeDtypeStruct((rows, width), F32)] * 2,
        compiler_params=pltpu.CompilerParams(vmem_limit_bytes=VMEM_LIMIT),
        cost_estimate=HEAVY,
        name="hole",
    )(h_rel, *a_list, *a_list)


def finish_kernel(where, *refs):
    keeps, (got, hole_a, hole_b, occ, energy, res, upd) = refs[:RING], refs[RING:]
    core = where[32]
    mine = pl.multiple_of(core * 32, 32)
    his = pl.multiple_of((1 - core) * 32, 32)
    for i in range(16):
        own = keeps[i // 4][i % 4 * 32:(i % 4 + 1) * 32, :256]
        for first, part, at in ((mine, own, i), (his, got[i * 32:(i + 1) * 32], 16 + i)):
            rows = pl.ds(first, 32)
            cols = pl.ds(pl.multiple_of(where[at] * 256, 256), 256)
            total = part + (hole_a[rows, cols] + hole_b[rows, cols])
            res[rows, cols] = total
            upd[rows, cols] = (total / (energy[:, cols] - occ[rows, :])).astype(BF)


def finish(where, keeps, got, hole_a, hole_b, occ, energy):
    shape = hole_a.shape
    vm = pl.BlockSpec(memory_space=pltpu.VMEM)
    return pl.pallas_call(
        finish_kernel,
        in_specs=[pl.BlockSpec(memory_space=pltpu.SMEM)] + [vm] * 9,
        out_specs=[vm, vm],
        out_shape=[jax.ShapeDtypeStruct(shape, F32), jax.ShapeDtypeStruct(shape, BF)],
        compiler_params=pltpu.CompilerParams(vmem_limit_bytes=VMEM_LIMIT),
        cost_estimate=LIGHT,
        name="finish",
    )(where, *keeps, got, hole_a, hole_b, occ, energy)


def local(amplitudes, ladder_ints, hole_ints, tile_irrep, pair_orbitals, occ_energy, pair_energy):
    z, y, x, c = (lax.axis_index(name) for name in AXES)
    rows, width = amplitudes.shape
    half = rows // 2
    p = z * RING + y

    mine = lax.dynamic_slice_in_dim(amplitudes, c * half, half, 0)
    theirs = other_core(lax.dynamic_slice_in_dim(amplitudes, (1 - c) * half, half, 0))
    own = jnp.concatenate([mine, theirs], axis=1)

    i = jnp.arange(16, dtype=jnp.int32)
    low, high = x ^ 1, RING - 1 - x
    first, second = jnp.where(c == 0, low, high), jnp.where(c == 0, high, low)
    goes = jnp.where(i < 4, x, jnp.where(i < 8, second, jnp.where(i < 12, first, (x + 2) % RING)))
    o = 2 * goes + (c + i // 2 % 2) % 2
    tile = o * 32 + 2 * p + i % 2
    t = jnp.arange(tile_irrep.shape[0], dtype=jnp.int32)
    label = jnp.sum(jnp.where(tile[:, None] == t[None, :], tile_irrep[None, :], 0), axis=1)
    m = jnp.arange(16, dtype=jnp.int32)
    v_of = 2 * x + (c + m // 4) % 2
    block = v_of * 4 + m % 4
    hit = (t[None, None, :] // 8 == block[None, :, None]) & (tile_irrep[None, None, :] == label[:, None, None])
    inside = jnp.sum(jnp.where(hit, t[None, None, :] % 8, 0), axis=2)
    offs = (m // 4 * 32 + m % 4 * 8)[None, :] + inside
    tab = jnp.where(m[None, :] < 8, offs, o[:, None]).reshape(256)

    hold = lax.optimization_barrier
    ints2d = ladder_ints.reshape(-1, ladder_ints.shape[2])

    quarter = half // 2
    r_m = along(own, True, 1)
    r_p = along(own, True, -1)
    w_a = select(hold((tab, own))[0], ints2d, 0)
    r_m, r_p, w_a, tab = hold((r_m, r_p, w_a, tab))
    s_a = jnp.concatenate([own, r_m, r_p[:quarter]], axis=0)
    q_ma = along(s_a, False, 1)
    q_pa = along(s_a, False, -1)
    r_2a = along(r_m[:quarter], True, 1)
    r_2b = along(r_p[quarter:], True, -1)
    w_b = select(tab, ints2d, 2)
    r_2a, r_2b, w_b = hold((r_2a, r_2b, w_b))
    s_b = jnp.concatenate([r_p[quarter:], r_2a, r_2b], axis=0)
    q_mb = along(s_b, False, 1)
    q_pb = along(s_b, False, -1)
    w_own = [w_a, w_b]
    w_other = [other_core(w) for w in w_own]

    i = jnp.arange(33, dtype=jnp.int32)
    kf = sum(jnp.where(i // 4 % 4 == k, jnp.int32(-RELS[k] % RING), 0) for k in range(RING))
    ks = sum(jnp.where(i % 4 == k, jnp.int32(RELS[k] % RING), 0) for k in range(RING))
    flip = (c + i // 16) % 2 == 0
    kz, ky = jnp.where(flip, ks, kf), jnp.where(flip, kf, ks)
    where = jnp.where(i == 32, c, (z + kz) % RING * RING + (y + ky) % RING)
    orbital = jnp.arange(occ_energy.shape[0], dtype=jnp.int32)
    picked = (pair_orbitals[:, :, None] == orbital[None, None, :]).astype(F32)
    occ = jnp.sum(picked * occ_energy[None, None, :], axis=(1, 2))[:, None]

    j = jnp.arange(16 * half, dtype=jnp.int32)
    ds = sum(jnp.where(j // (4 * half) == k, jnp.int32(RELS[k] % RING), 0) for k in range(RING))
    df = sum(jnp.where(j // half % 4 == k, jnp.int32(RELS[k] % RING), 0) for k in range(RING))
    dz, dy = jnp.where(c == 0, ds, df), jnp.where(c == 0, df, ds)
    source = ((z + dz) % RING * RING + (y + dy) % RING) * rows + c * half + j % half
    onehot = (jnp.arange(hole_ints.shape[1], dtype=jnp.int32)[:, None] == source[None, :]).astype(BF)
    h_rel = jnp.dot(hole_ints, onehot, preferred_element_type=F32).astype(BF)

    q_ma, q_pa, w_other, where, occ, h_rel = hold((q_ma, q_pa, w_other, where, occ, h_rel))
    q_2a = along(q_ma, False, 1)

    mid = 4 * TW
    block = RING * half

    def coded(value):
        return (value * SCALE).astype(F16)

    def decoded(value):
        return value.astype(F32) * (1.0 / SCALE)

    def halves(keep, got):
        total = keep + decoded(got)
        return total[:, :mid], coded(total[:, mid:])

    keep_0, send_0 = ladder(tab, [s_a, s_b], w_own, w_other)
    got_0 = across_x(send_0, True)
    q_pb, keep_0 = hold((q_pb, keep_0))
    q_2b = along(q_pb, False, -1)
    q_mb, got_0 = hold((q_mb, got_0))
    sum_0 = keep_0 + got_0
    end_0 = across_x(sum_0[:, mid:], False)
    a_list = [s_a, s_b, q_ma, q_mb, q_pa, q_pb, q_2a, q_2b]
    keep_1, send_1 = ladder(tab, a_list[2:6], w_own, w_other)
    got_1 = across_x(coded(send_1), True)
    keep_2, send_2 = ladder(tab, a_list[6:], w_own, w_other)
    got_1, keep_2, send_2 = hold((got_1, keep_2, send_2))
    sum_1, fwd_1 = halves(keep_1, got_1)
    end_1 = across_x(fwd_1, False)
    far_parts = [coded(keep_2[:, mid:]), coded(send_2[:, :mid]), coded(send_2[:, mid:])]
    far_got = [
        across_x(far_parts[0], False),
        across_x(far_parts[1], True),
        lax.ppermute(far_parts[2], "x", [(i, (i + 2) % RING) for i in range(RING)]),
    ]
    hole_own, hole_send = hole_part(h_rel, a_list, width)
    far_got, hole_send = hold((far_got, hole_send))
    t_0 = sum_0[:, :mid] + end_0
    t_m = sum_1[:block] + decoded(end_1[:block])
    t_p = sum_1[block:] + decoded(end_1[block:])
    t_2 = keep_2[:, :mid] + sum(decoded(part) for part in far_got)

    from_p = decoded(along(coded(t_m), False, -1))
    from_m = decoded(along(coded(t_p), False, 1))
    from_2 = decoded(along(coded(t_2), False, 2))
    from_p, from_m, from_2 = hold((from_p, from_m, from_2))
    hole_got = other_core(hole_send)
    back = [t_0, from_m, from_p, from_2]
    keeps = []
    for k in range(RING):
        u = jnp.concatenate([part[k * half:(k + 1) * half] for part in back], axis=0)
        keeps.append(u if k == 0 else along(u, True, RELS[k]))
    got = other_core(jnp.concatenate([u[:, mid // 2:] for u in keeps], axis=0))
    return finish(where, keeps, got, hole_own, hole_got, occ, pair_energy[None, :])


def solution(mesh):
    grid = Mesh(mesh.devices.reshape(RING, RING, RING, 2), AXES)
    pair, virt = ("z", "y"), ("x", "core")
    placed = (
        P(pair, virt),
        P(virt, None, pair),
        P(pair, None),
        P(),
        P(pair, None),
        P(),
        P(virt),
    )
    return jax.shard_map(
        local,
        mesh=grid,
        in_specs=placed,
        out_specs=(P(pair, virt), P(pair, virt)),
        check_vma=False,
    )
```

```python
import functools

import jax
import jax.numpy as jnp
from jax import lax
from jax.experimental import pallas as pl
from jax.experimental.pallas import tpu as pltpu
from jax.sharding import Mesh
from jax.sharding import PartitionSpec as P

TW = 128
RING = 4
AXES = ("z", "y", "x", "core")
BF = jnp.bfloat16
F32 = jnp.float32
VMEM_LIMIT = 24 * 1024 * 1024
SCALE = 64.0
F16 = jnp.float16
HEAVY = pl.CostEstimate(flops=2**36, bytes_accessed=2**26, transcendentals=0)
LIGHT = pl.CostEstimate(flops=1024, bytes_accessed=1024, transcendentals=0)
RELS = (0, -1, 1, 2)


def flat(z, y, x, c):
    return (((z % RING) * RING + y % RING) * RING + x % RING) * 2 + c


def perm_of(first, step):
    pairs = []
    for z in range(RING):
        for y in range(RING):
            for x in range(RING):
                for c in range(2):
                    if (c == 0) == first:
                        to = flat(z, y + step, x, c)
                    else:
                        to = flat(z + step, y, x, c)
                    pairs.append((flat(z, y, x, c), to))
    return pairs


def along(value, first, step):
    return lax.ppermute(value, AXES, perm_of(first, step))


def partner(x, c, first):
    return x ^ 1 if (c == 0) == first else RING - 1 - x


def across_x(value, first):
    pairs = []
    for z in range(RING):
        for y in range(RING):
            for x in range(RING):
                for c in range(2):
                    pairs.append((flat(z, y, x, c), flat(z, y, partner(x, c, first), c)))
    return lax.ppermute(value, AXES, pairs)


def other_core(value):
    return lax.ppermute(value, "core", [(0, 1), (1, 0)])


def select_kernel(tab, ints, out, held, sem, *, first_block):
    rows = 8 * 8 * TW
    copies = [
        pltpu.make_async_copy(ints.at[pl.ds((first_block + b) * rows, rows)], held.at[b], sem.at[b])
        for b in range(2)
    ]
    for cp in copies:
        cp.start()
    row = lax.broadcasted_iota(jnp.int32, (32, 256), 0)
    col = lax.broadcasted_iota(jnp.int32, (32, 256), 1)
    for b in range(2):
        copies[b].wait()
        for ct in range(16):
            pick = jnp.where(col == row * 8 + tab[ct * 16 + 8], 1.0, 0.0).astype(BF)
            tile = tab[ct * 16 + first_block + b] - (first_block + b) * 8
            for g in range(4):
                at = pl.multiple_of(tile * 8 * TW + g * 256, 256)
                got = jnp.dot(
                    pick, held[b, pl.ds(at, 256), ct % 2 * TW:(ct % 2 + 1) * TW], preferred_element_type=F32
                )
                out[ct, b * TW + g * 32:b * TW + (g + 1) * 32, :] = got.astype(BF)


def select(tab, ints2d, first_block):
    return pl.pallas_call(
        functools.partial(select_kernel, first_block=first_block),
        in_specs=[pl.BlockSpec(memory_space=pltpu.SMEM), pl.BlockSpec(memory_space=pltpu.HBM)],
        out_specs=pl.BlockSpec(memory_space=pltpu.VMEM),
        out_shape=jax.ShapeDtypeStruct((16, 2 * TW, TW), BF),
        scratch_shapes=[pltpu.VMEM((2, 8 * 8 * TW, 2 * TW), BF), pltpu.SemaphoreType.DMA((2,))],
        compiler_params=pltpu.CompilerParams(vmem_limit_bytes=50 * 1024 * 1024),
        cost_estimate=LIGHT,
        name="select",
    )(tab, ints2d)


def ladder_kernel(tab, *refs, n):
    a_refs, w_own, w_other, outs = refs[:n], refs[n:n + 2], refs[n + 2:n + 4], refs[n + 4:]
    for ct in range(16):
        d, q = ct // 4, ct % 4
        cols = [
            jnp.concatenate(
                [a[:, pl.ds(pl.multiple_of(tab[ct * 16 + m] * TW, TW), TW)] for a in a_refs], axis=0
            )
            for m in range(8)
        ]
        there = (0, 2, 1, 3)[d] * 4 + (q ^ 2)
        w = jnp.concatenate([w[ct] for w in w_own] + [w[there] for w in w_other], axis=0)
        got = jnp.dot(jnp.concatenate(cols, axis=1), w, preferred_element_type=F32)
        at = d % 2 * 4 + q
        outs[d // 2][:, at * TW:(at + 1) * TW] = got


def ladder(tab, a_list, w_own, w_other, cost=LIGHT):
    rows, n = sum(a.shape[0] for a in a_list), len(a_list)
    vm = pl.BlockSpec(memory_space=pltpu.VMEM)
    return pl.pallas_call(
        functools.partial(ladder_kernel, n=n),
        in_specs=[pl.BlockSpec(memory_space=pltpu.SMEM)] + [vm] * (n + 4),
        out_specs=[vm] * 2,
        out_shape=[jax.ShapeDtypeStruct((rows, 8 * TW), F32)] * 2,
        compiler_params=pltpu.CompilerParams(vmem_limit_bytes=VMEM_LIMIT),
        cost_estimate=cost,
        name="ladder",
    )(tab, *a_list, *w_own, *w_other)


def hole_kernel(h_ref, *refs):
    n = (len(refs) - 2) // 2
    for out, parts in ((refs[-2], refs[:n]), (refs[-1], refs[n:2 * n])):
        a = jnp.concatenate([r[...] for r in parts], axis=0)
        out[...] = jnp.dot(h_ref[...], a, preferred_element_type=F32)


def hole_part(h_rel, a_list, width):
    step = 1024
    steps = width // step
    rows = h_rel.shape[0]
    specs = [pl.BlockSpec((a.shape[0], step), lambda i: (0, i)) for a in a_list]
    specs2 = [pl.BlockSpec((a.shape[0], step), lambda i: (0, i + steps)) for a in a_list]
    return pl.pallas_call(
        hole_kernel,
        grid=(steps,),
        in_specs=[pl.BlockSpec(h_rel.shape, lambda i: (0, 0))] + specs + specs2,
        out_specs=[pl.BlockSpec((rows, step), lambda i: (0, i))] * 2,
        out_shape=[jax.ShapeDtypeStruct((rows, width), F32)] * 2,
        compiler_params=pltpu.CompilerParams(vmem_limit_bytes=VMEM_LIMIT),
        cost_estimate=HEAVY,
        name="hole",
    )(h_rel, *a_list, *a_list)


def finish_kernel(*refs):
    keeps, gots, (hole_a, hole_b, occ, energy, res, upd) = refs[:RING], refs[RING:2 * RING], refs[2 * RING:]
    z, y, core = (lax.axis_index(name) for name in ("z", "y", "core"))
    rows = occ.shape[1]
    square = (rows, rows)
    same = lax.broadcasted_iota(jnp.int32, square, 0) == lax.broadcasted_iota(jnp.int32, square, 1)
    occ_col = jnp.sum(jnp.where(same, occ[...], 0.0), axis=1, keepdims=True)
    low, high = occ_col[:32], occ_col[32:]
    occ_rows = [jnp.where(core == 0, low, high), jnp.where(core == 0, high, low)]
    for i in range(16):
        k, j = i // 4, i % 4
        for parts, lanes, sender in ((keeps, 0, core), (gots, 256, 1 - core)):
            kf, ks = -RELS[k] % RING, RELS[j] % RING
            kz, ky = jnp.where(sender == 0, ks, kf), jnp.where(sender == 0, kf, ks)
            col = lax.rem(z + kz, RING) * RING + lax.rem(y + ky, RING)
            at = pl.ds(pl.multiple_of(sender * 32, 32), 32)
            cols = pl.ds(pl.multiple_of(col * 256, 256), 256)
            total = parts[k][j * 32:(j + 1) * 32, lanes:lanes + 256] + (hole_a[at, cols] + hole_b[at, cols])
            res[at, cols] = total
            upd[at, cols] = (total / (energy[:, cols] - occ_rows[lanes // 256])).astype(BF)


def finish(keeps, gots, hole_a, hole_b, occ, energy):
    shape = hole_a.shape
    vm = pl.BlockSpec(memory_space=pltpu.VMEM)
    return pl.pallas_call(
        finish_kernel,
        in_specs=[vm] * 12,
        out_specs=[vm, vm],
        out_shape=[jax.ShapeDtypeStruct(shape, F32), jax.ShapeDtypeStruct(shape, BF)],
        compiler_params=pltpu.CompilerParams(vmem_limit_bytes=VMEM_LIMIT),
        cost_estimate=LIGHT,
        name="finish",
    )(*keeps, *gots, hole_a, hole_b, occ, energy)


def local(amplitudes, ladder_ints, hole_ints, tile_irrep, pair_orbitals, occ_energy, pair_energy):
    z, y, x, c = (lax.axis_index(name) for name in AXES)
    rows, width = amplitudes.shape
    half = rows // 2
    p = z * RING + y

    mine = lax.dynamic_slice_in_dim(amplitudes, c * half, half, 0)
    theirs = other_core(lax.dynamic_slice_in_dim(amplitudes, (1 - c) * half, half, 0))
    own = jnp.concatenate([mine, theirs], axis=1)

    i = jnp.arange(16, dtype=jnp.int32)
    low, high = x ^ 1, RING - 1 - x
    first, second = jnp.where(c == 0, low, high), jnp.where(c == 0, high, low)
    goes = jnp.where(i < 4, x, jnp.where(i < 8, second, jnp.where(i < 12, first, (x + 2) % RING)))
    o = 2 * goes + (c + i // 2 % 2) % 2
    tile = o * 32 + 2 * p + i % 2
    t = jnp.arange(tile_irrep.shape[0], dtype=jnp.int32)
    label = jnp.sum(jnp.where(tile[:, None] == t[None, :], tile_irrep[None, :], 0), axis=1)
    m = jnp.arange(16, dtype=jnp.int32)
    v_of = 2 * x + (c + m // 4) % 2
    block = v_of * 4 + m % 4
    hit = (t[None, None, :] // 8 == block[None, :, None]) & (tile_irrep[None, None, :] == label[:, None, None])
    inside = jnp.sum(jnp.where(hit, t[None, None, :] % 8, 0), axis=2)
    offs = (m // 4 * 32 + m % 4 * 8)[None, :] + inside
    tab = jnp.where(m[None, :] < 8, offs, o[:, None]).reshape(256)

    hold = lax.optimization_barrier
    ints2d = ladder_ints.reshape(-1, ladder_ints.shape[2])

    quarter = half // 2
    r_m = along(own, True, -1)
    r_p = along(own, True, 1)
    w_a = select(hold((tab, own))[0], ints2d, 0)
    r_m, r_p, w_a, tab = hold((r_m, r_p, w_a, tab))
    s_a = jnp.concatenate([own, r_m, r_p[:quarter]], axis=0)
    q_ma = along(s_a, False, -1)
    q_pa = along(s_a, False, 1)
    r_2a = along(r_m[:quarter], True, -1)
    r_2b = along(r_p[quarter:], True, 1)
    w_b = select(tab, ints2d, 2)
    r_2a, r_2b, w_b = hold((r_2a, r_2b, w_b))
    s_b = jnp.concatenate([r_p[quarter:], r_2a, r_2b], axis=0)
    q_mb = along(s_b, False, -1)
    q_pb = along(s_b, False, 1)
    w_own = [w_a, w_b]
    w_other = [other_core(w) for w in w_own]

    orbital = jnp.arange(occ_energy.shape[0], dtype=jnp.int32)
    picked = (pair_orbitals[:, :, None] == orbital[None, None, :]).astype(F32)
    occ = jnp.sum(picked * occ_energy[None, None, :], axis=(1, 2))

    j = jnp.arange(16 * half, dtype=jnp.int32)
    ds = sum(jnp.where(j // (4 * half) == k, jnp.int32(RELS[k] % RING), 0) for k in range(RING))
    df = sum(jnp.where(j // half % 4 == k, jnp.int32(-RELS[k] % RING), 0) for k in range(RING))
    dz, dy = jnp.where(c == 0, ds, df), jnp.where(c == 0, df, ds)
    source = ((z + dz) % RING * RING + (y + dy) % RING) * rows + c * half + j % half
    onehot = (jnp.arange(hole_ints.shape[1], dtype=jnp.int32)[:, None] == source[None, :]).astype(BF)
    h_rel = jnp.dot(hole_ints, onehot, preferred_element_type=F32).astype(BF)

    q_ma, q_pa, w_other, occ, h_rel = hold((q_ma, q_pa, w_other, occ, h_rel))
    q_2a = along(q_ma, False, -1)

    mid = 4 * TW
    block = RING * half

    def coded(value):
        return (value * SCALE).astype(F16)

    def decoded(value):
        return value.astype(F32) * (1.0 / SCALE)

    def halves(keep, got):
        total = keep + decoded(got)
        return total[:, :mid], coded(total[:, mid:])

    keep_0, send_0 = ladder(tab, [s_a, s_b], w_own, w_other)
    got_0 = across_x(send_0, True)
    q_pb, keep_0 = hold((q_pb, keep_0))
    q_2b = along(q_pb, False, 1)
    q_mb, got_0 = hold((q_mb, got_0))
    sum_0 = keep_0 + got_0
    end_0 = across_x(sum_0[:, mid:], False)
    a_list = [s_a, s_b, q_pa, q_pb, q_ma, q_mb, q_2a, q_2b]
    keep_1, send_1 = ladder(tab, a_list[2:6], w_own, w_other)
    got_1 = across_x(coded(send_1), True)
    keep_2, send_2 = ladder(tab, a_list[6:], w_own, w_other)
    got_1, keep_2, send_2 = hold((got_1, keep_2, send_2))
    sum_1, fwd_1 = halves(keep_1, got_1)
    end_1 = across_x(fwd_1, False)
    far_parts = [coded(keep_2[:, mid:]), coded(send_2[:, :mid]), coded(send_2[:, mid:])]
    far_got = [
        across_x(far_parts[0], False),
        across_x(far_parts[1], True),
        lax.ppermute(far_parts[2], "x", [(i, (i + 2) % RING) for i in range(RING)]),
    ]
    hole_own, hole_send = hole_part(h_rel, a_list, width)
    far_got, hole_send = hold((far_got, hole_send))
    t_0 = sum_0[:, :mid] + end_0
    t_m = sum_1[:block] + decoded(end_1[:block])
    t_p = sum_1[block:] + decoded(end_1[block:])
    t_2 = keep_2[:, :mid] + sum(decoded(part) for part in far_got)

    from_p = decoded(along(coded(t_m), False, -1))
    from_m = decoded(along(coded(t_p), False, 1))
    from_2 = decoded(along(coded(t_2), False, 2))
    from_p, from_m, from_2 = hold((from_p, from_m, from_2))
    hole_got = other_core(hole_send)
    back = [t_0, from_m, from_p, from_2]
    keeps = [jnp.concatenate([part[m * half:(m + 1) * half] for part in back], axis=0) for m in (0, 2, 1, 3)]
    gots = [other_core(keeps[0])]
    keeps[1], gots[0] = hold((keeps[1], gots[0]))
    for k in range(1, RING):
        keeps[k] = along(keeps[k], True, RELS[k])
        gots.append(other_core(keeps[k]))
    return finish(keeps, gots, hole_own, hole_got, occ[None, :], pair_energy[None, :])


def solution(mesh):
    grid = Mesh(mesh.devices.reshape(RING, RING, RING, 2), AXES)
    pair, virt = ("z", "y"), ("x", "core")
    placed = (
        P(pair, virt),
        P(virt, None, pair),
        P(pair, None),
        P(),
        P(pair, None),
        P(),
        P(virt),
    )
    return jax.shard_map(
        local,
        mesh=grid,
        in_specs=placed,
        out_specs=(P(pair, virt), P(pair, virt)),
        check_vma=False,
    )
```

```python
import functools

import jax
import jax.numpy as jnp
from jax import lax
from jax.experimental import pallas as pl
from jax.experimental.pallas import tpu as pltpu
from jax.sharding import Mesh
from jax.sharding import PartitionSpec as P

TW = 128
RING = 4
AXES = ("z", "y", "x", "core")
BF = jnp.bfloat16
F32 = jnp.float32
VMEM_LIMIT = 24 * 1024 * 1024
SCALE = 16.0
F16 = jnp.float16
HEAVY = pl.CostEstimate(flops=2**36, bytes_accessed=2**26, transcendentals=0)
LIGHT = pl.CostEstimate(flops=1024, bytes_accessed=1024, transcendentals=0)
RELS = (0, -1, 1, 2)


def flat(z, y, x, c):
    return (((z % RING) * RING + y % RING) * RING + x % RING) * 2 + c


def perm_of(first, step):
    pairs = []
    for z in range(RING):
        for y in range(RING):
            for x in range(RING):
                for c in range(2):
                    if (c == 0) == first:
                        to = flat(z, y + step, x, c)
                    else:
                        to = flat(z + step, y, x, c)
                    pairs.append((flat(z, y, x, c), to))
    return pairs


def along(value, first, step):
    return lax.ppermute(value, AXES, perm_of(first, step))


def partner(x, c, first):
    return x ^ 1 if (c == 0) == first else RING - 1 - x


def across_x(value, first):
    pairs = []
    for z in range(RING):
        for y in range(RING):
            for x in range(RING):
                for c in range(2):
                    pairs.append((flat(z, y, x, c), flat(z, y, partner(x, c, first), c)))
    return lax.ppermute(value, AXES, pairs)


def other_core(value):
    return lax.ppermute(value, "core", [(0, 1), (1, 0)])


def select_kernel(tab, ints, out, held, sem, *, first_block):
    rows = 8 * 8 * TW
    copies = [
        pltpu.make_async_copy(ints.at[pl.ds((first_block + b) * rows, rows)], held.at[b], sem.at[b])
        for b in range(2)
    ]
    for cp in copies:
        cp.start()
    row = lax.broadcasted_iota(jnp.int32, (32, 256), 0)
    col = lax.broadcasted_iota(jnp.int32, (32, 256), 1)
    for b in range(2):
        copies[b].wait()
        for ct in range(16):
            pick = jnp.where(col == row * 8 + tab[ct * 16 + 8], 1.0, 0.0).astype(BF)
            tile = tab[ct * 16 + first_block + b] - (first_block + b) * 8
            for g in range(4):
                at = pl.multiple_of(tile * 8 * TW + g * 256, 256)
                got = jnp.dot(
                    pick, held[b, pl.ds(at, 256), ct % 2 * TW:(ct % 2 + 1) * TW], preferred_element_type=F32
                )
                out[ct, b * TW + g * 32:b * TW + (g + 1) * 32, :] = got.astype(BF)


def select(tab, ints2d, first_block):
    return pl.pallas_call(
        functools.partial(select_kernel, first_block=first_block),
        in_specs=[pl.BlockSpec(memory_space=pltpu.SMEM), pl.BlockSpec(memory_space=pltpu.HBM)],
        out_specs=pl.BlockSpec(memory_space=pltpu.VMEM),
        out_shape=jax.ShapeDtypeStruct((16, 2 * TW, TW), BF),
        scratch_shapes=[pltpu.VMEM((2, 8 * 8 * TW, 2 * TW), BF), pltpu.SemaphoreType.DMA((2,))],
        compiler_params=pltpu.CompilerParams(vmem_limit_bytes=50 * 1024 * 1024),
        cost_estimate=LIGHT,
        name="select",
    )(tab, ints2d)


def ladder_kernel(tab, *refs, n):
    a_refs, w_own, w_other, outs = refs[:n], refs[n:n + 2], refs[n + 2:n + 4], refs[n + 4:]
    for ct in range(16):
        d, q = ct // 4, ct % 4
        cols = [
            jnp.concatenate(
                [a[:, pl.ds(pl.multiple_of(tab[ct * 16 + m] * TW, TW), TW)] for a in a_refs], axis=0
            )
            for m in range(8)
        ]
        there = (0, 2, 1, 3)[d] * 4 + (q ^ 2)
        w = jnp.concatenate([w[ct] for w in w_own] + [w[there] for w in w_other], axis=0)
        got = jnp.dot(jnp.concatenate(cols, axis=1), w, preferred_element_type=F32)
        at = d % 2 * 4 + q
        outs[d // 2][:, at * TW:(at + 1) * TW] = got


def ladder(tab, a_list, w_own, w_other, cost=LIGHT):
    rows, n = sum(a.shape[0] for a in a_list), len(a_list)
    vm = pl.BlockSpec(memory_space=pltpu.VMEM)
    return pl.pallas_call(
        functools.partial(ladder_kernel, n=n),
        in_specs=[pl.BlockSpec(memory_space=pltpu.SMEM)] + [vm] * (n + 4),
        out_specs=[vm] * 2,
        out_shape=[jax.ShapeDtypeStruct((rows, 8 * TW), F32)] * 2,
        compiler_params=pltpu.CompilerParams(vmem_limit_bytes=VMEM_LIMIT),
        cost_estimate=cost,
        name="ladder",
    )(tab, *a_list, *w_own, *w_other)


def hole_kernel(h_ref, *refs):
    n = (len(refs) - 2) // 2
    for out, parts in ((refs[-2], refs[:n]), (refs[-1], refs[n:2 * n])):
        a = jnp.concatenate([r[...] for r in parts], axis=0)
        out[...] = jnp.dot(h_ref[...], a, preferred_element_type=F32)


def hole_part(h_rel, a_list, width):
    step = 1024
    steps = width // step
    rows = h_rel.shape[0]
    specs = [pl.BlockSpec((a.shape[0], step), lambda i: (0, i)) for a in a_list]
    specs2 = [pl.BlockSpec((a.shape[0], step), lambda i: (0, i + steps)) for a in a_list]
    return pl.pallas_call(
        hole_kernel,
        grid=(steps,),
        in_specs=[pl.BlockSpec(h_rel.shape, lambda i: (0, 0))] + specs + specs2,
        out_specs=[pl.BlockSpec((rows, step), lambda i: (0, i))] * 2,
        out_shape=[jax.ShapeDtypeStruct((rows, width), F32)] * 2,
        compiler_params=pltpu.CompilerParams(vmem_limit_bytes=VMEM_LIMIT),
        cost_estimate=HEAVY,
        name="hole",
    )(h_rel, *a_list, *a_list)


def finish_kernel(*refs):
    keeps, gots, (hole_a, hole_b, occ, energy, res, upd) = refs[:RING], refs[RING:2 * RING], refs[2 * RING:]
    z, y, core = (lax.axis_index(name) for name in ("z", "y", "core"))
    rows = occ.shape[1]
    square = (rows, rows)
    same = lax.broadcasted_iota(jnp.int32, square, 0) == lax.broadcasted_iota(jnp.int32, square, 1)
    occ_col = jnp.sum(jnp.where(same, occ[...], 0.0), axis=1, keepdims=True)
    low, high = occ_col[:32], occ_col[32:]
    occ_rows = [jnp.where(core == 0, low, high), jnp.where(core == 0, high, low)]
    for i in range(16):
        k, j = i // 4, i % 4
        for parts, lanes, sender in ((keeps, 0, core), (gots, 256, 1 - core)):
            kf, ks = -RELS[k] % RING, RELS[j] % RING
            kz, ky = jnp.where(sender == 0, ks, kf), jnp.where(sender == 0, kf, ks)
            col = lax.rem(z + kz, RING) * RING + lax.rem(y + ky, RING)
            at = pl.ds(pl.multiple_of(sender * 32, 32), 32)
            cols = pl.ds(pl.multiple_of(col * 256, 256), 256)
            total = parts[k][j * 32:(j + 1) * 32, lanes:lanes + 256] + (hole_a[at, cols] + hole_b[at, cols])
            res[at, cols] = total
            upd[at, cols] = (total / (energy[:, cols] - occ_rows[lanes // 256])).astype(BF)


def finish(keeps, gots, hole_a, hole_b, occ, energy):
    shape = hole_a.shape
    vm = pl.BlockSpec(memory_space=pltpu.VMEM)
    return pl.pallas_call(
        finish_kernel,
        in_specs=[vm] * 12,
        out_specs=[vm, vm],
        out_shape=[jax.ShapeDtypeStruct(shape, F32), jax.ShapeDtypeStruct(shape, BF)],
        compiler_params=pltpu.CompilerParams(vmem_limit_bytes=VMEM_LIMIT),
        cost_estimate=LIGHT,
        name="finish",
    )(*keeps, *gots, hole_a, hole_b, occ, energy)


def local(amplitudes, ladder_ints, hole_ints, tile_irrep, pair_orbitals, occ_energy, pair_energy):
    z, y, x, c = (lax.axis_index(name) for name in AXES)
    rows, width = amplitudes.shape
    half = rows // 2
    p = z * RING + y

    mine = lax.dynamic_slice_in_dim(amplitudes, c * half, half, 0)
    theirs = other_core(lax.dynamic_slice_in_dim(amplitudes, (1 - c) * half, half, 0))
    own = jnp.concatenate([mine, theirs], axis=1)

    i = jnp.arange(16, dtype=jnp.int32)
    low, high = x ^ 1, RING - 1 - x
    first, second = jnp.where(c == 0, low, high), jnp.where(c == 0, high, low)
    goes = jnp.where(i < 4, x, jnp.where(i < 8, second, jnp.where(i < 12, first, (x + 2) % RING)))
    o = 2 * goes + (c + i // 2 % 2) % 2
    tile = o * 32 + 2 * p + i % 2
    t = jnp.arange(tile_irrep.shape[0], dtype=jnp.int32)
    label = jnp.sum(jnp.where(tile[:, None] == t[None, :], tile_irrep[None, :], 0), axis=1)
    m = jnp.arange(16, dtype=jnp.int32)
    v_of = 2 * x + (c + m // 4) % 2
    block = v_of * 4 + m % 4
    hit = (t[None, None, :] // 8 == block[None, :, None]) & (tile_irrep[None, None, :] == label[:, None, None])
    inside = jnp.sum(jnp.where(hit, t[None, None, :] % 8, 0), axis=2)
    offs = (m // 4 * 32 + m % 4 * 8)[None, :] + inside
    tab = jnp.where(m[None, :] < 8, offs, o[:, None]).reshape(256)

    hold = lax.optimization_barrier
    ints2d = ladder_ints.reshape(-1, ladder_ints.shape[2])

    quarter = half // 2
    r_m = along(own, True, -1)
    r_p = along(own, True, 1)
    w_a = select(hold((tab, own))[0], ints2d, 0)
    r_m, r_p, w_a, tab = hold((r_m, r_p, w_a, tab))
    s_a = jnp.concatenate([own, r_m, r_p[:quarter]], axis=0)
    q_ma = along(s_a, False, -1)
    q_pa = along(s_a, False, 1)
    r_2a = along(r_m[:quarter], True, -1)
    r_2b = along(r_p[quarter:], True, 1)
    w_b = select(tab, ints2d, 2)
    r_2a, r_2b, w_b = hold((r_2a, r_2b, w_b))
    s_b = jnp.concatenate([r_p[quarter:], r_2a, r_2b], axis=0)
    q_mb = along(s_b, False, -1)
    q_pb = along(s_b, False, 1)
    w_own = [w_a, w_b]
    w_other = [other_core(w) for w in w_own]

    orbital = jnp.arange(occ_energy.shape[0], dtype=jnp.int32)
    picked = (pair_orbitals[:, :, None] == orbital[None, None, :]).astype(F32)
    occ = jnp.sum(picked * occ_energy[None, None, :], axis=(1, 2))

    j = jnp.arange(16 * half, dtype=jnp.int32)
    ds = sum(jnp.where(j // (4 * half) == k, jnp.int32(RELS[k] % RING), 0) for k in range(RING))
    df = sum(jnp.where(j // half % 4 == k, jnp.int32(-RELS[k] % RING), 0) for k in range(RING))
    dz, dy = jnp.where(c == 0, ds, df), jnp.where(c == 0, df, ds)
    source = ((z + dz) % RING * RING + (y + dy) % RING) * rows + c * half + j % half
    onehot = (jnp.arange(hole_ints.shape[1], dtype=jnp.int32)[:, None] == source[None, :]).astype(BF)
    h_rel = jnp.dot(hole_ints, onehot, preferred_element_type=F32).astype(BF)

    q_ma, q_pa, w_other, occ, h_rel = hold((q_ma, q_pa, w_other, occ, h_rel))
    q_2a = along(q_ma, False, -1)

    mid = 4 * TW
    block = RING * half

    def coded(value):
        return (value * SCALE).astype(F16)

    def decoded(value):
        return value.astype(F32) * (1.0 / SCALE)

    def halves(keep, got):
        total = keep + decoded(got)
        return total[:, :mid], coded(total[:, mid:])

    keep_0, send_0 = ladder(tab, [s_a, s_b], w_own, w_other)
    got_0 = across_x(send_0, True)
    q_pb, keep_0 = hold((q_pb, keep_0))
    q_2b = along(q_pb, False, 1)
    q_mb, got_0 = hold((q_mb, got_0))
    sum_0 = keep_0 + got_0
    end_0 = across_x(sum_0[:, mid:], False)
    a_list = [s_a, s_b, q_pa, q_pb, q_ma, q_mb, q_2a, q_2b]
    keep_1, send_1 = ladder(tab, a_list[2:6], w_own, w_other)
    got_1 = across_x(coded(send_1), True)
    keep_2, send_2 = ladder(tab, a_list[6:], w_own, w_other)
    got_1, keep_2, send_2 = hold((got_1, keep_2, send_2))
    sum_1, fwd_1 = halves(keep_1, got_1)
    end_1 = across_x(fwd_1, False)
    far_parts = [coded(keep_2[:, mid:]), coded(send_2[:, :mid]), coded(send_2[:, mid:])]
    far_got = [
        across_x(far_parts[0], False),
        across_x(far_parts[1], True),
        lax.ppermute(far_parts[2], "x", [(i, (i + 2) % RING) for i in range(RING)]),
    ]
    hole_own, hole_send = hole_part(h_rel, a_list, width)
    far_got, hole_send = hold((far_got, hole_send))
    t_0 = sum_0[:, :mid] + end_0
    t_m = sum_1[:block] + decoded(end_1[:block])
    t_p = sum_1[block:] + decoded(end_1[block:])
    t_2 = keep_2[:, :mid] + sum(decoded(part) for part in far_got)

    from_p = decoded(along(coded(t_m), False, -1))
    from_m = decoded(along(coded(t_p), False, 1))
    from_2 = decoded(along(coded(t_2), False, 2))
    from_p, from_m, from_2 = hold((from_p, from_m, from_2))
    hole_got = other_core(hole_send)
    back = [t_0, from_m, from_p, from_2]
    keeps = [jnp.concatenate([part[m * half:(m + 1) * half] for part in back], axis=0) for m in (0, 2, 1, 3)]
    gots = [other_core(keeps[0])]
    keeps[1], gots[0] = hold((keeps[1], gots[0]))
    for k in range(1, RING):
        keeps[k] = along(keeps[k], True, RELS[k])
        gots.append(other_core(keeps[k]))
    return finish(keeps, gots, hole_own, hole_got, occ[None, :], pair_energy[None, :])


def solution(mesh):
    grid = Mesh(mesh.devices.reshape(RING, RING, RING, 2), AXES)
    pair, virt = ("z", "y"), ("x", "core")
    placed = (
        P(pair, virt),
        P(virt, None, pair),
        P(pair, None),
        P(),
        P(pair, None),
        P(),
        P(virt),
    )
    return jax.shard_map(
        local,
        mesh=grid,
        in_specs=placed,
        out_specs=(P(pair, virt), P(pair, virt)),
        check_vma=False,
    )
```

```python
import functools

import jax
import jax.numpy as jnp
from jax import lax
from jax.experimental import pallas as pl
from jax.experimental.pallas import tpu as pltpu
from jax.sharding import Mesh
from jax.sharding import PartitionSpec as P

TW = 128
RING = 4
AXES = ("z", "y", "x", "core")
BF = jnp.bfloat16
F32 = jnp.float32
VMEM_LIMIT = 24 * 1024 * 1024
SCALE = 16.0
F16 = jnp.float16
HEAVY = pl.CostEstimate(flops=2**36, bytes_accessed=2**26, transcendentals=0)
LIGHT = pl.CostEstimate(flops=1024, bytes_accessed=1024, transcendentals=0)
RELS = (0, -1, 1, 2)


def flat(z, y, x, c):
    return (((z % RING) * RING + y % RING) * RING + x % RING) * 2 + c


def perm_of(first, step):
    pairs = []
    for z in range(RING):
        for y in range(RING):
            for x in range(RING):
                for c in range(2):
                    if (c == 0) == first:
                        to = flat(z, y + step, x, c)
                    else:
                        to = flat(z + step, y, x, c)
                    pairs.append((flat(z, y, x, c), to))
    return pairs


def along(value, first, step):
    return lax.ppermute(value, AXES, perm_of(first, step))


def partner(x, c, first):
    return x ^ 1 if (c == 0) == first else RING - 1 - x


def across_x(value, first):
    pairs = []
    for z in range(RING):
        for y in range(RING):
            for x in range(RING):
                for c in range(2):
                    pairs.append((flat(z, y, x, c), flat(z, y, partner(x, c, first), c)))
    return lax.ppermute(value, AXES, pairs)


def other_core(value):
    return lax.ppermute(value, "core", [(0, 1), (1, 0)])


def select_kernel(tab, ints, out, held, sem, *, first_block):
    rows = 8 * 8 * TW
    copies = [
        pltpu.make_async_copy(ints.at[pl.ds((first_block + b) * rows, rows)], held.at[b], sem.at[b])
        for b in range(2)
    ]
    for cp in copies:
        cp.start()
    row = lax.broadcasted_iota(jnp.int32, (32, 256), 0)
    col = lax.broadcasted_iota(jnp.int32, (32, 256), 1)
    for b in range(2):
        copies[b].wait()
        for ct in range(16):
            pick = jnp.where(col == row * 8 + tab[ct * 16 + 8], 1.0, 0.0).astype(BF)
            tile = tab[ct * 16 + first_block + b] - (first_block + b) * 8
            for g in range(4):
                at = pl.multiple_of(tile * 8 * TW + g * 256, 256)
                got = jnp.dot(
                    pick, held[b, pl.ds(at, 256), ct % 2 * TW:(ct % 2 + 1) * TW], preferred_element_type=F32
                )
                out[ct, b * TW + g * 32:b * TW + (g + 1) * 32, :] = got.astype(BF)


def select(tab, ints2d, first_block):
    return pl.pallas_call(
        functools.partial(select_kernel, first_block=first_block),
        in_specs=[pl.BlockSpec(memory_space=pltpu.SMEM), pl.BlockSpec(memory_space=pltpu.HBM)],
        out_specs=pl.BlockSpec(memory_space=pltpu.VMEM),
        out_shape=jax.ShapeDtypeStruct((16, 2 * TW, TW), BF),
        scratch_shapes=[pltpu.VMEM((2, 8 * 8 * TW, 2 * TW), BF), pltpu.SemaphoreType.DMA((2,))],
        compiler_params=pltpu.CompilerParams(vmem_limit_bytes=50 * 1024 * 1024),
        cost_estimate=LIGHT,
        name="select",
    )(tab, ints2d)


def ladder_kernel(tab, *refs, n):
    a_refs, w_own, w_other, outs = refs[:n], refs[n:n + 2], refs[n + 2:n + 4], refs[n + 4:]
    for ct in range(16):
        d, q = ct // 4, ct % 4
        cols = [
            jnp.concatenate(
                [a[:, pl.ds(pl.multiple_of(tab[ct * 16 + m] * TW, TW), TW)] for a in a_refs], axis=0
            )
            for m in range(8)
        ]
        there = (0, 2, 1, 3)[d] * 4 + (q ^ 2)
        w = jnp.concatenate([w[ct] for w in w_own] + [w[there] for w in w_other], axis=0)
        got = jnp.dot(jnp.concatenate(cols, axis=1), w, preferred_element_type=F32)
        at = d % 2 * 4 + q
        outs[d // 2][:, at * TW:(at + 1) * TW] = got


def ladder(tab, a_list, w_own, w_other, cost=LIGHT):
    rows, n = sum(a.shape[0] for a in a_list), len(a_list)
    vm = pl.BlockSpec(memory_space=pltpu.VMEM)
    return pl.pallas_call(
        functools.partial(ladder_kernel, n=n),
        in_specs=[pl.BlockSpec(memory_space=pltpu.SMEM)] + [vm] * (n + 4),
        out_specs=[vm] * 2,
        out_shape=[jax.ShapeDtypeStruct((rows, 8 * TW), F32)] * 2,
        compiler_params=pltpu.CompilerParams(vmem_limit_bytes=VMEM_LIMIT),
        cost_estimate=cost,
        name="ladder",
    )(tab, *a_list, *w_own, *w_other)


def hole_kernel(h_ref, *refs):
    n = (len(refs) - 2) // 2
    for out, parts in ((refs[-2], refs[:n]), (refs[-1], refs[n:2 * n])):
        a = jnp.concatenate([r[...] for r in parts], axis=0)
        out[...] = jnp.dot(h_ref[...], a, preferred_element_type=F32)


def hole_part(h_rel, a_list, width):
    step = 1024
    steps = width // step
    rows = h_rel.shape[0]
    specs = [pl.BlockSpec((a.shape[0], step), lambda i: (0, i)) for a in a_list]
    specs2 = [pl.BlockSpec((a.shape[0], step), lambda i: (0, i + steps)) for a in a_list]
    return pl.pallas_call(
        hole_kernel,
        grid=(steps,),
        in_specs=[pl.BlockSpec(h_rel.shape, lambda i: (0, 0))] + specs + specs2,
        out_specs=[pl.BlockSpec((rows, step), lambda i: (0, i))] * 2,
        out_shape=[jax.ShapeDtypeStruct((rows, width), F32)] * 2,
        compiler_params=pltpu.CompilerParams(vmem_limit_bytes=VMEM_LIMIT),
        cost_estimate=HEAVY,
        name="hole",
    )(h_rel, *a_list, *a_list)


def finish_kernel(*refs):
    keeps, gots, (hole_a, hole_b, occ, energy, res, upd) = refs[:RING], refs[RING:2 * RING], refs[2 * RING:]
    z, y, core = (lax.axis_index(name) for name in ("z", "y", "core"))
    rows = occ.shape[1]
    square = (rows, rows)
    same = lax.broadcasted_iota(jnp.int32, square, 0) == lax.broadcasted_iota(jnp.int32, square, 1)
    occ_col = jnp.sum(jnp.where(same, occ[...], 0.0), axis=1, keepdims=True)
    low, high = occ_col[:32], occ_col[32:]
    occ_rows = [jnp.where(core == 0, low, high), jnp.where(core == 0, high, low)]
    for i in range(16):
        k, j = i // 4, i % 4
        for parts, lanes, sender in ((keeps, 0, core), (gots, 256, 1 - core)):
            kf, ks = -RELS[k] % RING, RELS[j] % RING
            kz, ky = jnp.where(sender == 0, ks, kf), jnp.where(sender == 0, kf, ks)
            col = lax.rem(z + kz, RING) * RING + lax.rem(y + ky, RING)
            at = pl.ds(pl.multiple_of(sender * 32, 32), 32)
            cols = pl.ds(pl.multiple_of(col * 256, 256), 256)
            total = parts[k][j * 32:(j + 1) * 32, lanes:lanes + 256] + (hole_a[at, cols] + hole_b[at, cols])
            res[at, cols] = total
            upd[at, cols] = (total / (energy[:, cols] - occ_rows[lanes // 256])).astype(BF)


def finish(keeps, gots, hole_a, hole_b, occ, energy):
    shape = hole_a.shape
    vm = pl.BlockSpec(memory_space=pltpu.VMEM)
    return pl.pallas_call(
        finish_kernel,
        in_specs=[vm] * 12,
        out_specs=[vm, vm],
        out_shape=[jax.ShapeDtypeStruct(shape, F32), jax.ShapeDtypeStruct(shape, BF)],
        compiler_params=pltpu.CompilerParams(vmem_limit_bytes=VMEM_LIMIT),
        cost_estimate=LIGHT,
        name="finish",
    )(*keeps, *gots, hole_a, hole_b, occ, energy)


def local(amplitudes, ladder_ints, hole_ints, tile_irrep, pair_orbitals, occ_energy, pair_energy):
    z, y, x, c = (lax.axis_index(name) for name in AXES)
    rows, width = amplitudes.shape
    half = rows // 2
    p = z * RING + y

    mine = lax.dynamic_slice_in_dim(amplitudes, c * half, half, 0)
    theirs = other_core(lax.dynamic_slice_in_dim(amplitudes, (1 - c) * half, half, 0))
    own = jnp.concatenate([mine, theirs], axis=1)

    i = jnp.arange(16, dtype=jnp.int32)
    low, high = x ^ 1, RING - 1 - x
    first, second = jnp.where(c == 0, low, high), jnp.where(c == 0, high, low)
    goes = jnp.where(i < 4, x, jnp.where(i < 8, second, jnp.where(i < 12, first, (x + 2) % RING)))
    o = 2 * goes + (c + i // 2 % 2) % 2
    tile = o * 32 + 2 * p + i % 2
    t = jnp.arange(tile_irrep.shape[0], dtype=jnp.int32)
    label = jnp.sum(jnp.where(tile[:, None] == t[None, :], tile_irrep[None, :], 0), axis=1)
    m = jnp.arange(16, dtype=jnp.int32)
    v_of = 2 * x + (c + m // 4) % 2
    block = v_of * 4 + m % 4
    hit = (t[None, None, :] // 8 == block[None, :, None]) & (tile_irrep[None, None, :] == label[:, None, None])
    inside = jnp.sum(jnp.where(hit, t[None, None, :] % 8, 0), axis=2)
    offs = (m // 4 * 32 + m % 4 * 8)[None, :] + inside
    tab = jnp.where(m[None, :] < 8, offs, o[:, None]).reshape(256)

    hold = lax.optimization_barrier
    ints2d = ladder_ints.reshape(-1, ladder_ints.shape[2])

    quarter = half // 2
    r_m = along(own, True, -1)
    r_p = along(own, True, 1)
    w_a = select(hold((tab, own))[0], ints2d, 0)
    r_m, r_p, w_a, tab = hold((r_m, r_p, w_a, tab))
    s_a = jnp.concatenate([own, r_m, r_p[:quarter]], axis=0)
    q_ma = along(s_a, False, -1)
    q_pa = along(s_a, False, 1)
    r_2a = along(r_m[:quarter], True, -1)
    r_2b = along(r_p[quarter:], True, 1)
    w_b = select(tab, ints2d, 2)
    r_2a, r_2b, w_b = hold((r_2a, r_2b, w_b))
    s_b = jnp.concatenate([r_p[quarter:], r_2a, r_2b], axis=0)
    q_mb = along(s_b, False, -1)
    q_pb = along(s_b, False, 1)
    w_own = [w_a, w_b]
    w_other = [other_core(w) for w in w_own]

    orbital = jnp.arange(occ_energy.shape[0], dtype=jnp.int32)
    picked = (pair_orbitals[:, :, None] == orbital[None, None, :]).astype(F32)
    occ = jnp.sum(picked * occ_energy[None, None, :], axis=(1, 2))

    j = jnp.arange(16 * half, dtype=jnp.int32)
    ds = sum(jnp.where(j // (4 * half) == k, jnp.int32(RELS[k] % RING), 0) for k in range(RING))
    df = sum(jnp.where(j // half % 4 == k, jnp.int32(-RELS[k] % RING), 0) for k in range(RING))
    dz, dy = jnp.where(c == 0, ds, df), jnp.where(c == 0, df, ds)
    source = ((z + dz) % RING * RING + (y + dy) % RING) * rows + c * half + j % half
    onehot = (jnp.arange(hole_ints.shape[1], dtype=jnp.int32)[:, None] == source[None, :]).astype(BF)
    h_rel = jnp.dot(hole_ints, onehot, preferred_element_type=F32).astype(BF)

    q_ma, q_pa, w_other, occ, h_rel = hold((q_ma, q_pa, w_other, occ, h_rel))
    q_2a = along(q_ma, False, -1)

    mid = 4 * TW
    block = RING * half

    def coded(value):
        return (value * SCALE).astype(F16)

    def decoded(value):
        return value.astype(F32) * (1.0 / SCALE)

    def halves(keep, got):
        total = keep + decoded(got)
        return total[:, :mid], coded(total[:, mid:])

    keep_0, send_0 = ladder(tab, [s_a, s_b], w_own, w_other)
    got_0 = across_x(send_0, True)
    q_pb, keep_0 = hold((q_pb, keep_0))
    q_2b = along(q_pb, False, 1)
    q_mb, got_0 = hold((q_mb, got_0))
    sum_0 = keep_0 + got_0
    end_0 = across_x(sum_0[:, mid:], False)
    a_list = [s_a, s_b, q_pa, q_pb, q_ma, q_mb, q_2a, q_2b]
    keep_1, send_1 = ladder(tab, a_list[2:6], w_own, w_other)
    got_1 = across_x(coded(send_1), True)
    keep_2, send_2 = ladder(tab, a_list[6:], w_own, w_other)
    got_1 = hold((got_1, keep_2, send_2))[0]
    sum_1, fwd_1 = halves(keep_1, got_1)
    end_1 = across_x(fwd_1, False)
    far_parts = [coded(keep_2[:, mid:]), coded(send_2[:, :mid]), coded(send_2[:, mid:])]
    far_got = [
        across_x(far_parts[0], False),
        across_x(far_parts[1], True),
        lax.ppermute(far_parts[2], "x", [(i, (i + 2) % RING) for i in range(RING)]),
    ]
    hole_own, hole_send = hole_part(h_rel, a_list, width)
    far_got, hole_send = hold((far_got, hole_send))
    t_0 = sum_0[:, :mid] + end_0
    t_m = sum_1[:block] + decoded(end_1[:block])
    t_p = sum_1[block:] + decoded(end_1[block:])
    t_2 = keep_2[:, :mid] + sum(decoded(part) for part in far_got)

    from_p = decoded(along(coded(t_m), False, -1))
    from_m = decoded(along(coded(t_p), False, 1))
    from_2 = decoded(along(coded(t_2), False, 2))
    from_p, from_m, from_2 = hold((from_p, from_m, from_2))
    hole_got = other_core(hole_send)
    back = [t_0, from_m, from_p, from_2]
    keeps = [jnp.concatenate([part[m * half:(m + 1) * half] for part in back], axis=0) for m in (0, 2, 1, 3)]
    gots = [other_core(keeps[0])]
    keeps[1], gots[0] = hold((keeps[1], gots[0]))
    for k in range(1, RING):
        keeps[k] = along(keeps[k], True, RELS[k])
        gots.append(other_core(keeps[k]))
    return finish(keeps, gots, hole_own, hole_got, occ[None, :], pair_energy[None, :])


def solution(mesh):
    grid = Mesh(mesh.devices.reshape(RING, RING, RING, 2), AXES)
    pair, virt = ("z", "y"), ("x", "core")
    placed = (
        P(pair, virt),
        P(virt, None, pair),
        P(pair, None),
        P(),
        P(pair, None),
        P(),
        P(virt),
    )
    return jax.shard_map(
        local,
        mesh=grid,
        in_specs=placed,
        out_specs=(P(pair, virt), P(pair, virt)),
        check_vma=False,
    )
```
